512 devices in a mesh: replica: 16 (over x, z_lo), fsdp: 32 (over z_hi, y, core).
Axes of the slice: x: 4, y: 8, z: 8 (z_hi: 2, z_lo: 4; z = z_hi * 4 + z_lo), core: 2. Of those that a mesh axis runs over, the one named last changes fastest.
Arguments:
- activations: bfloat16 [16, 4096, 8192], P('replica', 'fsdp'), as said below
- norm_gain: float32 [16, 8192], P('replica'), may hold values from 0.1 to 1.9
- key_weight: bfloat16 [16, 8192, 512], P('replica', 'fsdp'), may hold values from -0.0625 to 0.0625
- key_cotangent: bfloat16 [16, 4096, 512], P('replica', 'fsdp'), as said below
- fragment_local: bfloat16 [16, 8192, 512], P('replica', 'fsdp'), may hold values from -6 to 6
- outer_params: float32 [8192, 512], P(('fsdp', 'replica')), may hold values from -6 to 6
- outer_momentum: float32 [8192, 512], P(('fsdp', 'replica')), may hold values from -3 to 3
Outputs:
- keys: bfloat16 [16, 4096, 512], P('replica', 'fsdp')
- weight_grad: bfloat16 [16, 8192, 512], P('replica', 'fsdp')
- gain_grad: float32 [16, 8192], P('replica')
- new_params: float32 [8192, 512], P(('fsdp', 'replica'))
- new_momentum: float32 [8192, 512], P(('fsdp', 'replica'))
The draws below stay inside these ranges and needn't reach their ends.
Inputs may be any that keep to these rules, and one draw needn't show every extreme that they name: `activations`: independent entries; rows have scales of 1 to 16 and feature columns scales of 1 to 10. `key_cotangent`: independent entries whose scale varies with the token.
All inputs are finite; a program needn't handle non-finite values.
Results may differ from the reference program's by a relative error of at most 0.0049.
Values may be sent and summed in bfloat16 or wider, within the bound.
No kernel may reach another device: no remote copies, remote signals or barrier semaphores. Data moves between devices by JAX's collectives and lax.ppermute only.
A program may use at most 64 MiB of HBM per device.

```python
import math
import jax
import jax.numpy as jnp
from jax import lax

D = 8192
KD = 512
GROUP_TOKENS = 4096
N_REPLICA = 16


def draw_activations(key, part):
    key = jax.random.fold_in(key, 11)
    first, second, third = jax.random.split(key, 3)
    shape = (N_REPLICA, GROUP_TOKENS, D)
    column_scale = jnp.exp(jax.random.uniform(second, (1, 1, D), jnp.float32) * math.log(10.0))
    row_scale = jnp.exp(jax.random.uniform(first, (N_REPLICA, GROUP_TOKENS, 1), jnp.float32) * math.log(10.0))
    base = jax.random.normal(third, shape, jnp.float32)
    return (base * row_scale * column_scale).astype(jnp.bfloat16)


def draw_key_cotangent(key, part):
    key = jax.random.fold_in(key, 23)
    first = jax.random.fold_in(key, 0)
    shape = (N_REPLICA, GROUP_TOKENS, KD)
    position = jnp.arange(GROUP_TOKENS, dtype=jnp.float32) / (GROUP_TOKENS - 1)
    ramp = (0.02 * (1.0 + 2.0 * position))[None, :, None]
    base = jax.random.normal(first, shape, jnp.float32)
    return (base * ramp).astype(jnp.bfloat16)


def spiked(result, own_key, source, target, shards_of, factor):
    owner, partner = [(jnp.arange(result.shape[dim]) // (result.shape[dim] // shards_of)).reshape([-1 if axis == dim else 1 for axis in range(result.ndim)]) for dim in (source, target)]
    chosen = jax.random.permutation(own_key, shards_of)[partner]
    strong = (owner == chosen) | (owner == (partner + shards_of // 2) % shards_of)
    return jnp.where(strong, factor * result, result)


def levels(key, extent, cuts, low, top_value):
    def one(axis_at, shards_of):
        draws = jax.random.uniform(jax.random.fold_in(jax.random.fold_in(key, 6), axis_at), (shards_of,), jnp.float32, low / len(cuts), top_value / len(cuts))
        return jnp.repeat(jnp.exp(draws), extent[axis_at] // shards_of).reshape((-1,) + (1,) * (len(extent) - axis_at - 1))

    level = one(*cuts[0])
    for cut in cuts[1:]:
        level = level * one(*cut)
    return level


def centred(key, shape, scale, most, cuts=(), kind=jnp.bfloat16):
    result = scale * jax.random.normal(key, shape, jnp.float32)
    if cuts:
        result = result * levels(key, shape, cuts, -0.22, 0.18)
    return jnp.clip(result, -most, most).astype(kind)


def gaussian_with(stream_key, shape, spread, reach, shards, heavy, kind=jnp.bfloat16):
    entries = spread * jax.random.normal(stream_key, shape, jnp.float32)
    if shards:
        entries = entries * levels(stream_key, shape, shards, -0.22, 0.18)
    return jnp.clip(spiked(entries, jax.random.fold_in(stream_key, 3), *heavy), -reach, reach).astype(kind)


def setup_inputs(seed: int = 0) -> dict:
    splits = jax.random.split(jax.random.key(seed), 8)
    return {
        "activations": draw_activations(jax.random.fold_in(splits[7], 71), 0),
        "norm_gain": jnp.clip(1.0 + 0.18 * jax.random.normal(splits[1], (N_REPLICA, D), jnp.float32), 0.1, 1.9),
        "key_weight": centred(splits[2], (N_REPLICA, D, KD), D ** -0.5, 0.0625, ((0, 16), (1, 32))),
        "key_cotangent": draw_key_cotangent(jax.random.fold_in(splits[7], 71), 0),
        "fragment_local": gaussian_with(splits[4], (N_REPLICA, D, KD), 1.0, 6.0, ((0, 16), (1, 32)), (0, 1, 16, 2.0)),
        "outer_params": centred(splits[5], (D, KD), 1.0, 6.0, ((0, 512),), jnp.float32),
        "outer_momentum": centred(splits[6], (D, KD), 0.5, 3.0, ((0, 512),), jnp.float32),
    }


epsilon = 1e-05

def one_group(activations, norm_gain, key_weight, key_cotangent):
    values = activations.astype(jnp.float32)
    inverse = lax.rsqrt(lax.optimization_barrier(jnp.mean(values * values, axis=1, keepdims=True)) + epsilon)
    normed = values * inverse
    hidden = (normed * norm_gain[None, :]).astype(jnp.bfloat16)
    keys = jnp.dot(hidden, key_weight, preferred_element_type=jnp.float32).astype(jnp.bfloat16)
    hidden_grad = lax.dot_general(key_cotangent, key_weight, (((1,), (1,)), ((), ())), preferred_element_type=jnp.float32)
    gain_grad = lax.optimization_barrier(jnp.sum(hidden_grad * normed, axis=0))
    weight_grad = lax.dot_general(hidden, key_cotangent, (((0,), (0,)), ((), ())), preferred_element_type=jnp.float32).astype(jnp.bfloat16)
    return (keys, weight_grad, gain_grad)

def reference(activations, norm_gain, key_weight, key_cotangent, fragment_local, outer_params, outer_momentum):
    key_list = []
    grad_list = []
    gain_list = []
    for group in range(N_REPLICA):
        keys, weight_grad, gain_grad = one_group(activations[group], norm_gain[group], key_weight[group], key_cotangent[group])
        key_list.append(keys)
        grad_list.append(weight_grad)
        gain_list.append(gain_grad)
    local_mean = lax.optimization_barrier(jnp.sum(fragment_local.astype(jnp.float32), axis=0)) / N_REPLICA
    pseudo_grad = outer_params - local_mean
    new_momentum = 0.9 * outer_momentum + pseudo_grad
    new_params = outer_params - 0.7 * (pseudo_grad + 0.9 * new_momentum)
    return (jnp.stack(key_list), jnp.stack(grad_list), jnp.stack(gain_list), new_params, new_momentum)
```

```python
import jax
import jax.numpy as jnp
from jax import lax
from jax.sharding import PartitionSpec as P

epsilon = 1e-05


def body(
    activations, norm_gain, key_weight, key_cotangent, fragment_local, outer_params, outer_momentum
):
    values = activations[0].astype(jnp.float32)
    inverse = lax.rsqrt(jnp.mean(values * values, axis=1, keepdims=True) + epsilon)
    normed = values * inverse
    hidden = (normed * norm_gain[0][None, :]).astype(jnp.bfloat16)
    upstream = key_cotangent[0]
    weight_rows = key_weight[0]
    groups = lax.axis_size("fsdp")
    rows = weight_rows.shape[0]
    columns = lax.all_to_all(hidden, "fsdp", split_axis=1, concat_axis=0, tiled=True)
    all_upstream = lax.all_gather(upstream, "fsdp", axis=0, tiled=True)
    gathered = lax.all_gather(weight_rows, "fsdp", axis=0, tiled=True)

    pieces = lax.all_to_all(
        fragment_local[0], "replica", split_axis=0, concat_axis=0, tiled=True
    )
    replicas = lax.axis_size("replica")
    share_rows = outer_params.shape[0]
    own_share = jnp.sum(
        pieces.reshape(replicas, share_rows, -1).astype(jnp.float32), axis=0
    )
    pseudo_grad = outer_params - own_share / replicas
    new_momentum = 0.9 * outer_momentum + pseudo_grad
    new_params = outer_params - 0.7 * (pseudo_grad + 0.9 * new_momentum)

    grad_rows = lax.dot_general(
        columns, all_upstream, (((0,), (0,)), ((), ())), preferred_element_type=jnp.float32
    )
    own_gain = lax.dynamic_slice_in_dim(
        norm_gain[0], lax.axis_index("fsdp") * rows, rows, 0
    )
    own_terms = jnp.sum(grad_rows * weight_rows.astype(jnp.float32), axis=1) / own_gain
    gain_total = lax.all_to_all(
        jnp.broadcast_to(own_terms[None], (groups, rows)), "fsdp", 0, 0, tiled=True
    ).reshape(1, groups * rows)
    key_values = jnp.dot(hidden, gathered, preferred_element_type=jnp.float32)
    key_out = key_values.astype(jnp.bfloat16)[None]
    grad_out = grad_rows.astype(jnp.bfloat16)[None]
    return (key_out, grad_out, gain_total, new_params, new_momentum)


def solution(mesh):
    placed = (
        P("replica", "fsdp", None),
        P("replica", None),
        P("replica", "fsdp", None),
        P("replica", "fsdp", None),
        P("replica", "fsdp", None),
        P(("fsdp", "replica"), None),
        P(("fsdp", "replica"), None),
    )
    return jax.shard_map(
        body,
        mesh=mesh,
        in_specs=placed,
        out_specs=(
            P("replica", "fsdp", None),
            P("replica", "fsdp", None),
            P("replica", None),
            P(("fsdp", "replica"), None),
            P(("fsdp", "replica"), None),
        ),
        check_vma=False,
    )
```

```python
import jax
import jax.numpy as jnp
from jax import lax
from jax.experimental import pallas as pl
from jax.experimental.pallas import tpu as pltpu
from jax.sharding import Mesh, PartitionSpec as P

epsilon = 1e-05
F32 = jnp.float32
BF16 = jnp.bfloat16
FSDP = ("z", "y", "core")


def norm_kernel(place, x_ref, gain_ref, out_ref):
    slots, _, width = out_ref.shape
    part = width // 4
    half = x_ref.shape[1] // 2
    values = x_ref[...].astype(F32)
    total = jnp.sum(values * values, axis=1, keepdims=True)
    inverse = lax.rsqrt(total / x_ref.shape[1] + epsilon)
    for slot in range(slots):
        for piece in range(4):
            z = place[0] ^ (piece & 1)
            core = place[1] ^ (piece >> 1)
            start = pl.multiple_of(z * half + slot * 2 * part + core * part, part)
            block = x_ref[:, pl.ds(start, part)].astype(F32)
            scale = gain_ref[:, pl.ds(start, part)]
            out_ref[slot, :, piece * part:(piece + 1) * part] = (
                (block * inverse) * scale
            ).astype(out_ref.dtype)


def norm(place, x, gain, slots):
    tokens, width = x.shape
    rows = 32
    return pl.pallas_call(
        norm_kernel,
        out_shape=jax.ShapeDtypeStruct((slots, tokens, width // slots), BF16),
        grid_spec=pltpu.PrefetchScalarGridSpec(
            num_scalar_prefetch=1,
            grid=(tokens // rows,),
            in_specs=[
                pl.BlockSpec((rows, width), lambda i, place: (i, 0)),
                pl.BlockSpec((1, width), lambda i, place: (0, 0)),
            ],
            out_specs=pl.BlockSpec((slots, rows, width // slots), lambda i, place: (0, i, 0)),
        ),
        compiler_params=pltpu.CompilerParams(vmem_limit_bytes=32 * 1024 * 1024),
        cost_estimate=pl.CostEstimate(
            flops=6 * tokens * width, bytes_accessed=4 * tokens * width, transcendentals=tokens
        ),
    )(place, x, gain)


def swap(x, axis):
    return lax.ppermute(x, axis, [(0, 1), (1, 0)])


def body(
    activations, norm_gain, key_weight, key_cotangent, fragment_local, outer_params, outer_momentum
):
    slots = lax.axis_size("y")
    z, core = lax.axis_index("z"), lax.axis_index("core")
    place = jnp.stack([z, core]).astype(jnp.int32)
    weight = key_weight[0]
    upstream = key_cotangent[0]
    part, keys = weight.shape
    tokens = upstream.shape[0]

    weight_two = jnp.concatenate([weight, swap(weight, "z")], axis=0)
    weight_slot = jnp.concatenate([weight_two, swap(weight_two, "core")], axis=0)

    hidden = norm(place, activations[0], norm_gain, slots)
    columns = lax.all_to_all(hidden, "y", 0, 0, tiled=True).reshape(slots * tokens, 4 * part)
    all_upstream = lax.all_gather(upstream, "y", axis=0, tiled=True)

    key_terms = jnp.dot(columns, weight_slot, preferred_element_type=F32).astype(BF16)
    key_parts = lax.all_to_all(key_terms, "y", 0, 0, tiled=True)
    key_out = jnp.sum(key_parts.reshape(slots, tokens, keys).astype(F32), axis=0).astype(BF16)

    contract = (((0,), (0,)), ((), ()))
    far = lax.dot_general(
        columns[:, 2 * part:], all_upstream, contract, preferred_element_type=F32
    )
    near = lax.dot_general(
        columns[:, :2 * part], all_upstream, contract, preferred_element_type=F32
    )
    chip = near + swap(far, "core")
    grad_rows = chip[:part] + swap(chip[part:].astype(BF16), "z").astype(F32)

    terms = jnp.concatenate(
        [
            jnp.sum(near * weight_slot[:2 * part].astype(F32), axis=1),
            jnp.sum(far * weight_slot[2 * part:].astype(F32), axis=1),
        ]
    )
    devices = 4 * slots
    spread = lax.all_to_all(
        jnp.broadcast_to(terms[None], (devices, 4 * part)), FSDP, 0, 0, tiled=True
    ).reshape(2, slots, 2, 2, 2, part)
    total = [
        [
            sum(
                spread[a, :, b, core_to ^ b, z_to ^ a]
                for a in range(2)
                for b in range(2)
            )
            for core_to in range(2)
        ]
        for z_to in range(2)
    ]
    gain_total = jnp.stack([jnp.stack(t, axis=1) for t in total]).reshape(1, -1) / norm_gain

    pieces = lax.all_to_all(fragment_local[0], "replica", 0, 0, tiled=True)
    replicas = lax.axis_size("replica")
    own_share = jnp.sum(
        pieces.reshape(replicas, outer_params.shape[0], -1).astype(F32), axis=0
    )
    pseudo_grad = outer_params - own_share / replicas
    new_momentum = 0.9 * outer_momentum + pseudo_grad
    new_params = outer_params - 0.7 * (pseudo_grad + 0.9 * new_momentum)
    return (key_out[None], grad_rows.astype(BF16)[None], gain_total, new_params, new_momentum)


def solution(mesh):
    shape = mesh.devices.shape
    split = Mesh(
        mesh.devices.reshape(shape[0], 2, shape[1] // 4, 2), ("replica",) + FSDP
    )
    rows = P("replica", FSDP, None)
    share = P(FSDP + ("replica",), None)
    return jax.shard_map(
        body,
        mesh=split,
        in_specs=(rows, P("replica", None), rows, rows, rows, share, share),
        out_specs=(rows, rows, P("replica", None), share, share),
        check_vma=False,
    )
```

```python
import jax
import jax.numpy as jnp
from jax import lax
from jax.experimental import pallas as pl
from jax.experimental.pallas import tpu as pltpu
from jax.sharding import Mesh, PartitionSpec as P

epsilon = 1e-05
F32 = jnp.float32
BF16 = jnp.bfloat16
FSDP = ("z", "y", "core")
VMEM_LIMIT = 48 * 1024 * 1024


def norm_kernel(place, x_ref, gain_ref, weight_ref, local_ref, weight_out, local_out, *out_refs):
    weight_out[...] = weight_ref[...]
    local_out[...] = local_ref[...]
    slots = len(out_refs)
    part = out_refs[0].shape[1] // 4
    half = x_ref.shape[1] // 2
    values = x_ref[...].astype(F32)
    total = jnp.sum(values * values, axis=1, keepdims=True)
    inverse = lax.rsqrt(total / x_ref.shape[1] + epsilon)
    for step in range(slots):
        slot = lax.rem(place[2] + step, slots)
        for piece in range(4):
            z = place[0] ^ (piece & 1)
            core = place[1] ^ (piece >> 1)
            start = pl.multiple_of(z * half + slot * 2 * part + core * part, part)
            block = x_ref[:, pl.ds(start, part)].astype(F32)
            scale = gain_ref[:, pl.ds(start, part)]
            out_refs[step][:, piece * part:(piece + 1) * part] = (
                (block * inverse) * scale
            ).astype(BF16)


def norm(place, x, gain, weight, local, slots):
    tokens, width = x.shape
    rows = 32
    steps = tokens // rows
    handed = pl.BlockSpec((weight.shape[0] // steps, weight.shape[1]), lambda i, place: (i, 0))
    return pl.pallas_call(
        norm_kernel,
        out_shape=[jax.ShapeDtypeStruct(weight.shape, BF16)] * 2
        + [jax.ShapeDtypeStruct((tokens, width // slots), BF16)] * slots,
        grid_spec=pltpu.PrefetchScalarGridSpec(
            num_scalar_prefetch=1,
            grid=(steps,),
            in_specs=[
                pl.BlockSpec((rows, width), lambda i, place: (i, 0)),
                pl.BlockSpec((1, width), lambda i, place: (0, 0)),
                handed,
                handed,
            ],
            out_specs=[handed] * 2
            + [pl.BlockSpec((rows, width // slots), lambda i, place: (i, 0))] * slots,
        ),
        compiler_params=pltpu.CompilerParams(vmem_limit_bytes=VMEM_LIMIT),
        cost_estimate=pl.CostEstimate(
            flops=6 * tokens * width, bytes_accessed=4 * tokens * width, transcendentals=tokens
        ),
    )(place, x, gain, weight, local)


def key_kernel(place, *refs):
    blocks, weights, (_, out_ref) = refs[:-6], refs[-6:-2], refs[-2:]
    slots, tokens = len(blocks), blocks[0].shape[0]
    values = jnp.concatenate([block[...] for block in blocks], axis=0)
    weight = jnp.concatenate([ref[...] for ref in weights], axis=0)
    terms = jnp.dot(values, weight, preferred_element_type=F32)
    for step in range(slots):
        source = lax.rem(place[2] + slots - step, slots)
        out_ref[source] = terms[step * tokens:(step + 1) * tokens]


def key_products(place, blocks, weights, before):
    slots, tokens = len(blocks), blocks[0].shape[0]
    part, keys = weights[0].shape
    return pl.pallas_call(
        key_kernel,
        out_shape=jax.ShapeDtypeStruct((slots, tokens, keys), F32),
        in_specs=[pl.BlockSpec(memory_space=pltpu.SMEM)]
        + [pl.BlockSpec(memory_space=pltpu.VMEM)] * (slots + 4)
        + [pl.BlockSpec(memory_space=pl.ANY)],
        out_specs=pl.BlockSpec(memory_space=pltpu.VMEM),
        compiler_params=pltpu.CompilerParams(vmem_limit_bytes=VMEM_LIMIT),
        cost_estimate=pl.CostEstimate(
            flops=8 * slots * tokens * part * keys, bytes_accessed=6 << 20, transcendentals=0
        ),
    )(place, *blocks, *weights, before)


def grad_part(place, blocks, upstream_ref, weights, first):
    slots = len(blocks)
    width = 2 * weights[0].shape[0]
    values = jnp.concatenate([block[:, first:first + width] for block in blocks], axis=0)
    upstream = jnp.concatenate(
        [upstream_ref[lax.rem(place[2] + slots - step, slots)] for step in range(slots)], axis=0
    )
    grad = lax.dot_general(
        values, upstream, (((0,), (0,)), ((), ())), preferred_element_type=F32
    )
    products = grad * jnp.concatenate([ref[...] for ref in weights], axis=0).astype(F32)
    terms = lax.dot_general(
        jnp.ones((8, products.shape[1]), F32),
        products,
        (((1,), (1,)), ((), ())),
        precision=lax.Precision.HIGHEST,
        preferred_element_type=F32,
    )
    return grad, terms


def far_kernel(place, *refs):
    blocks, (upstream_ref, *weights, _), (grad_ref, term_ref) = refs[:-6], refs[-6:-2], refs[-2:]
    grad_ref[...], term_ref[...] = grad_part(
        place, blocks, upstream_ref, weights, 2 * weights[0].shape[0]
    )


def near_kernel(place, *refs):
    blocks, (upstream_ref, *weights, other_ref), (own_ref, send_ref, term_ref) = (
        refs[:-7], refs[-7:-3], refs[-3:]
    )
    grad, term_ref[...] = grad_part(place, blocks, upstream_ref, weights, 0)
    chip = grad + other_ref[...]
    part = own_ref.shape[0]
    own_ref[...] = chip[:part]
    send_ref[...] = chip[part:].astype(BF16)


def grad_products(place, blocks, upstream, weights, before=None, other=None):
    slots, tokens = len(blocks), blocks[0].shape[0]
    part, keys = weights[0].shape
    terms = jax.ShapeDtypeStruct((8, 2 * part), F32)
    if other is None:
        shapes = (jax.ShapeDtypeStruct((2 * part, keys), F32), terms)
    else:
        shapes = (
            jax.ShapeDtypeStruct((part, keys), F32),
            jax.ShapeDtypeStruct((part, keys), BF16),
            terms,
        )
    in_vmem = pl.BlockSpec(memory_space=pltpu.VMEM)
    return pl.pallas_call(
        far_kernel if other is None else near_kernel,
        out_shape=shapes,
        in_specs=[pl.BlockSpec(memory_space=pltpu.SMEM)]
        + [in_vmem] * (slots + 3)
        + [pl.BlockSpec(memory_space=pl.ANY) if other is None else in_vmem],
        out_specs=(in_vmem,) * len(shapes),
        compiler_params=pltpu.CompilerParams(vmem_limit_bytes=VMEM_LIMIT),
        cost_estimate=pl.CostEstimate(
            flops=4 * slots * tokens * part * keys, bytes_accessed=5 << 20, transcendentals=0
        ),
    )(place, *blocks, upstream, *weights, before if other is None else other)


def swap(x, axis):
    return lax.ppermute(x, axis, [(0, 1), (1, 0)])


def body(
    activations, norm_gain, key_weight, key_cotangent, fragment_local, outer_params, outer_momentum
):
    slots = lax.axis_size("y")
    place = jnp.stack([lax.axis_index(name) for name in ("z", "core", "y")]).astype(jnp.int32)
    upstream = key_cotangent[0]
    part, keys = key_weight.shape[1:]
    tokens = upstream.shape[0]

    all_upstream = lax.all_gather(upstream, "y", axis=0, tiled=True).reshape(slots, tokens, keys)
    weight, local, *hidden = norm(
        place, activations[0], norm_gain, key_weight[0], fragment_local[0], slots
    )
    blocks = [hidden[0]] + [
        lax.ppermute(hidden[step], "y", [(i, (i + step) % slots) for i in range(slots)])
        for step in range(1, slots)
    ]
    weights = [
        weight,
        swap(weight, "z"),
        swap(weight, "core"),
        lax.ppermute(weight, ("z", "core"), [(i, 3 - i) for i in range(4)]),
    ]
    pieces = lax.all_to_all(local, "replica", 0, 0, tiled=True)

    key_terms = key_products(place, blocks, weights, pieces)
    key_out = lax.psum_scatter(
        key_terms.reshape(slots * tokens, keys), "y", scatter_dimension=0, tiled=True
    ).astype(BF16)

    far, far_terms = grad_products(place, blocks, all_upstream, weights[2:], before=key_terms)
    own, send, near_terms = grad_products(
        place, blocks, all_upstream, weights[:2], other=swap(far, "core")
    )
    grad_rows = own + swap(send, "z").astype(F32)

    terms = jnp.concatenate([near_terms[0], far_terms[0]])
    devices = 4 * slots
    spread = lax.all_to_all(
        jnp.broadcast_to(terms[None], (devices, 4 * part)), FSDP, 0, 0, tiled=True
    ).reshape(2, slots, 2, 2, 2, part)
    total = [
        [
            sum(
                spread[a, :, b, core_to ^ b, z_to ^ a]
                for a in range(2)
                for b in range(2)
            )
            for core_to in range(2)
        ]
        for z_to in range(2)
    ]
    gain_total = jnp.stack([jnp.stack(t, axis=1) for t in total]).reshape(1, -1) / norm_gain

    replicas = lax.axis_size("replica")
    own_share = jnp.sum(
        pieces.reshape(replicas, outer_params.shape[0], -1).astype(F32), axis=0
    )
    pseudo_grad = outer_params - own_share / replicas
    new_momentum = 0.9 * outer_momentum + pseudo_grad
    new_params = outer_params - 0.7 * (pseudo_grad + 0.9 * new_momentum)
    return (key_out[None], grad_rows.astype(BF16)[None], gain_total, new_params, new_momentum)


def solution(mesh):
    shape = mesh.devices.shape
    split = Mesh(
        mesh.devices.reshape(shape[0], 2, shape[1] // 4, 2), ("replica",) + FSDP
    )
    rows = P("replica", FSDP, None)
    share = P(FSDP + ("replica",), None)
    return jax.shard_map(
        body,
        mesh=split,
        in_specs=(rows, P("replica", None), rows, rows, rows, share, share),
        out_specs=(rows, rows, P("replica", None), share, share),
        check_vma=False,
    )
```

```python
import jax
import jax.numpy as jnp
from jax import lax
from jax.experimental import pallas as pl
from jax.experimental.pallas import tpu as pltpu
from jax.sharding import Mesh, PartitionSpec as P

epsilon = 1e-05
F32 = jnp.float32
BF16 = jnp.bfloat16
REPLICA = ("x", "depth")
FSDP = ("z", "y", "core")
VMEM_LIMIT = 48 * 1024 * 1024
NORM_VMEM_LIMIT = 60 * 1024 * 1024


def norm_kernel(place, x_ref, gain_ref, out_ref):
    slots, _, width = out_ref.shape
    part = width // 4
    half = x_ref.shape[1] // 2
    values = x_ref[...].astype(F32)
    total = jnp.sum(values * values, axis=1, keepdims=True)
    inverse = lax.rsqrt(total / x_ref.shape[1] + epsilon)
    for slot in range(slots):
        for piece in range(4):
            z = place[0] ^ (piece & 1)
            core = place[1] ^ (piece >> 1)
            start = pl.multiple_of(z * half + slot * 2 * part + core * part, part)
            block = x_ref[:, pl.ds(start, part)].astype(F32)
            scale = gain_ref[:, pl.ds(start, part)]
            out_ref[slot, :, piece * part:(piece + 1) * part] = (
                (block * inverse) * scale
            ).astype(out_ref.dtype)


def norm(place, x, gain, slots):
    tokens, width = x.shape
    rows = 32
    return pl.pallas_call(
        norm_kernel,
        out_shape=jax.ShapeDtypeStruct((slots, tokens, width // slots), BF16),
        grid_spec=pltpu.PrefetchScalarGridSpec(
            num_scalar_prefetch=1,
            grid=(tokens // rows,),
            in_specs=[
                pl.BlockSpec((rows, width), lambda i, place: (i, 0)),
                pl.BlockSpec((1, width), lambda i, place: (0, 0)),
            ],
            out_specs=pl.BlockSpec((slots, rows, width // slots), lambda i, place: (0, i, 0)),
        ),
        compiler_params=pltpu.CompilerParams(vmem_limit_bytes=NORM_VMEM_LIMIT),
        cost_estimate=pl.CostEstimate(
            flops=6 * tokens * width, bytes_accessed=4 * tokens * width, transcendentals=tokens
        ),
    )(place, x, gain)


def key_kernel(columns_ref, near_ref, far_ref, _, out_ref):
    slots, tokens, width = columns_ref.shape
    weight = jnp.concatenate([near_ref[...], far_ref[...]], axis=0)
    terms = jnp.dot(
        columns_ref[...].reshape(slots * tokens, width), weight, preferred_element_type=F32
    )
    out_ref[...] = terms.astype(out_ref.dtype)


def key_products(columns, weights, before, dtype):
    slots, tokens, width = columns.shape
    keys = weights[0].shape[1]
    in_vmem = pl.BlockSpec(memory_space=pltpu.VMEM)
    return pl.pallas_call(
        key_kernel,
        out_shape=jax.ShapeDtypeStruct((slots * tokens, keys), dtype),
        in_specs=[in_vmem] * 3 + [pl.BlockSpec(memory_space=pl.ANY)],
        out_specs=in_vmem,
        compiler_params=pltpu.CompilerParams(vmem_limit_bytes=VMEM_LIMIT),
        cost_estimate=pl.CostEstimate(
            flops=2 * slots * tokens * width * keys, bytes_accessed=5 << 20, transcendentals=0
        ),
    )(columns, *weights, before)


def grad_kernel(columns_ref, upstream_ref, _, near_ref, far_ref):
    slots, tokens, width = columns_ref.shape
    half = width // 2
    upstream = upstream_ref[...]
    for index, out_ref in ((1, far_ref), (0, near_ref)):
        values = columns_ref[:, :, index * half:(index + 1) * half]
        out_ref[...] = lax.dot_general(
            values.reshape(slots * tokens, half),
            upstream,
            (((0,), (0,)), ((), ())),
            preferred_element_type=F32,
        )


def grad_products(columns, upstream, before):
    slots, tokens, width = columns.shape
    keys = upstream.shape[1]
    in_vmem = pl.BlockSpec(memory_space=pltpu.VMEM)
    return pl.pallas_call(
        grad_kernel,
        out_shape=[jax.ShapeDtypeStruct((width // 2, keys), F32)] * 2,
        in_specs=[in_vmem] * 2 + [pl.BlockSpec(memory_space=pl.ANY)],
        out_specs=[in_vmem] * 2,
        compiler_params=pltpu.CompilerParams(vmem_limit_bytes=VMEM_LIMIT),
        cost_estimate=pl.CostEstimate(
            flops=2 * slots * tokens * width * keys, bytes_accessed=6 << 20, transcendentals=0
        ),
    )(columns, upstream, before)


def term_kernel(near_ref, far_ref, near_weight_ref, far_weight_ref, out_ref):
    half = near_ref.shape[0]
    for index, (grad_ref, weight_ref) in enumerate(
        ((near_ref, near_weight_ref), (far_ref, far_weight_ref))
    ):
        products = grad_ref[...] * weight_ref[...].astype(F32)
        out_ref[:, index * half:(index + 1) * half] = lax.dot_general(
            jnp.ones((8, products.shape[1]), F32),
            products,
            (((1,), (1,)), ((), ())),
            precision=lax.Precision.HIGHEST,
            preferred_element_type=F32,
        )


def term_rows(near, far, weights):
    in_vmem = pl.BlockSpec(memory_space=pltpu.VMEM)
    return pl.pallas_call(
        term_kernel,
        out_shape=jax.ShapeDtypeStruct((8, 2 * near.shape[0]), F32),
        in_specs=[in_vmem] * 4,
        out_specs=in_vmem,
        compiler_params=pltpu.CompilerParams(vmem_limit_bytes=32 * 1024 * 1024),
        cost_estimate=pl.CostEstimate(
            flops=16 * near.size, bytes_accessed=4 << 20, transcendentals=0
        ),
    )(near, far, *weights)


def chip_kernel(near_ref, other_ref, terms_ref, own_ref, send_ref, terms_out):
    part = own_ref.shape[0]
    own_ref[...] = near_ref[:part] + other_ref[:part]
    send_ref[...] = (near_ref[part:] + other_ref[part:]).astype(BF16)
    terms_out[...] = terms_ref[...]


def chip_sums(near, other, terms):
    part, keys = near.shape[0] // 2, near.shape[1]
    return pl.pallas_call(
        chip_kernel,
        out_shape=(
            jax.ShapeDtypeStruct((part, keys), F32),
            jax.ShapeDtypeStruct((part, keys), BF16),
            jax.ShapeDtypeStruct(terms.shape, F32),
        ),
        compiler_params=pltpu.CompilerParams(vmem_limit_bytes=16 * 1024 * 1024),
        cost_estimate=pl.CostEstimate(
            flops=near.size, bytes_accessed=10 * near.size, transcendentals=0
        ),
    )(near, other, terms)


def swap(x, axis):
    return lax.ppermute(x, axis, [(0, 1), (1, 0)])


def halved(rows, axis, bit):
    half = rows.shape[0] // 2
    upper = (lax.axis_index(axis) & bit) != 0
    sent = jnp.where(upper, rows[:half], rows[half:])
    kept = jnp.where(upper, rows[half:], rows[:half])
    size = lax.axis_size(axis)
    received = lax.ppermute(sent, axis, [(i, i ^ bit) for i in range(size)])
    return kept.astype(F32) + received.astype(F32)


def body(
    activations, norm_gain, key_weight, key_cotangent, fragment_local, outer_params, outer_momentum
):
    slots = lax.axis_size("y")
    z, core = lax.axis_index("z"), lax.axis_index("core")
    place = jnp.stack([z, core]).astype(jnp.int32)
    weight = key_weight[0]
    upstream = key_cotangent[0]
    part, keys = weight.shape
    tokens = upstream.shape[0]

    all_upstream = lax.all_gather(upstream, "y", axis=0, tiled=True)
    hidden = norm(place, activations[0], norm_gain, slots)
    columns = lax.all_to_all(hidden, "y", 0, 0, tiled=True)

    near_weight = jnp.concatenate([weight, swap(weight, "z")], axis=0)
    weights = [near_weight, swap(near_weight, "core")]

    own_share = fragment_local[0]
    for axis in REPLICA:
        for bit in (2, 1):
            own_share = halved(own_share, axis, bit)
    pseudo_grad = outer_params - own_share / (lax.axis_size("x") * lax.axis_size("depth"))
    new_momentum = 0.9 * outer_momentum + pseudo_grad
    new_params = outer_params - 0.7 * (pseudo_grad + 0.9 * new_momentum)

    key_terms = key_products(columns, weights, new_params, BF16)
    key_out = lax.psum_scatter(key_terms, "y", scatter_dimension=0, tiled=True).astype(BF16)

    near, far = grad_products(columns, all_upstream, key_terms)
    terms = term_rows(near, far, weights)
    own, send, terms = chip_sums(near, swap(far, "core"), terms)
    grad_rows = own + swap(send, "z").astype(F32)

    devices = 4 * slots
    spread = lax.all_to_all(
        jnp.broadcast_to(terms[:1], (devices, 4 * part)), FSDP, 0, 0, tiled=True
    ).reshape(2, slots, 2, 2, 2, part)
    total = [
        [
            sum(
                spread[a, :, b, core_to ^ b, z_to ^ a]
                for a in range(2)
                for b in range(2)
            )
            for core_to in range(2)
        ]
        for z_to in range(2)
    ]
    gain_total = jnp.stack([jnp.stack(t, axis=1) for t in total]).reshape(1, -1) / norm_gain
    return (key_out[None], grad_rows.astype(BF16)[None], gain_total, new_params, new_momentum)


def solution(mesh):
    replicas, devices = mesh.devices.shape
    split = Mesh(
        mesh.devices.reshape(replicas // 4, 4, 2, devices // 4, 2), REPLICA + FSDP
    )
    rows = P(REPLICA, FSDP, None)
    share = P(FSDP + REPLICA, None)
    return jax.shard_map(
        body,
        mesh=split,
        in_specs=(rows, P(REPLICA, None), rows, rows, rows, share, share),
        out_specs=(rows, rows, P(REPLICA, None), share, share),
        check_vma=False,
    )
```

```python
import jax
import jax.numpy as jnp
from jax import lax
from jax.experimental import pallas as pl
from jax.experimental.pallas import tpu as pltpu
from jax.sharding import Mesh, PartitionSpec as P

epsilon = 1e-05
F32 = jnp.float32
BF16 = jnp.bfloat16
REPLICA = ("x", "depth")
FSDP = ("z", "y", "core")
VMEM_LIMIT = 48 * 1024 * 1024
NORM_VMEM_LIMIT = 60 * 1024 * 1024


def norm_kernel(x_ref, gain_ref, out_ref):
    slots, _, width = out_ref.shape
    part = width // 4
    half = x_ref.shape[1] // 2
    values = x_ref[...].astype(F32)
    total = jnp.sum(values * values, axis=1, keepdims=True)
    inverse = lax.rsqrt(total / x_ref.shape[1] + epsilon)
    for slot in range(slots):
        for piece in range(4):
            z = lax.axis_index("z") ^ (piece & 1)
            core = lax.axis_index("core") ^ (piece >> 1)
            start = pl.multiple_of(z * half + slot * 2 * part + core * part, part)
            block = x_ref[:, pl.ds(start, part)].astype(F32)
            scale = gain_ref[:, pl.ds(start, part)]
            out_ref[slot, :, piece * part:(piece + 1) * part] = (
                (block * inverse) * scale
            ).astype(out_ref.dtype)


def norm(x, gain, slots):
    tokens, width = x.shape
    rows = 64
    return pl.pallas_call(
        norm_kernel,
        out_shape=jax.ShapeDtypeStruct((slots, tokens, width // slots), BF16),
        grid=(tokens // rows,),
        in_specs=[
            pl.BlockSpec((rows, width), lambda i: (i, 0)),
            pl.BlockSpec((1, width), lambda i: (0, 0)),
        ],
        out_specs=pl.BlockSpec((slots, rows, width // slots), lambda i: (0, i, 0)),
        compiler_params=pltpu.CompilerParams(vmem_limit_bytes=NORM_VMEM_LIMIT),
        cost_estimate=pl.CostEstimate(
            flops=6 * tokens * width, bytes_accessed=4 * tokens * width, transcendentals=tokens
        ),
    )(x, gain)


def key_kernel(columns_ref, near_ref, far_ref, _, out_ref):
    slots, tokens, width = columns_ref.shape
    weight = jnp.concatenate([near_ref[...], far_ref[...]], axis=0)
    terms = jnp.dot(
        columns_ref[...].reshape(slots * tokens, width), weight, preferred_element_type=F32
    )
    out_ref[...] = terms.astype(out_ref.dtype)


def key_products(columns, weights, before):
    slots, tokens, width = columns.shape
    keys = weights[0].shape[1]
    in_vmem = pl.BlockSpec(memory_space=pltpu.VMEM)
    return pl.pallas_call(
        key_kernel,
        out_shape=jax.ShapeDtypeStruct((slots * tokens, keys), BF16),
        in_specs=[in_vmem] * 3 + [pl.BlockSpec(memory_space=pl.ANY)],
        out_specs=in_vmem,
        compiler_params=pltpu.CompilerParams(vmem_limit_bytes=VMEM_LIMIT),
        cost_estimate=pl.CostEstimate(
            flops=2 * slots * tokens * width * keys, bytes_accessed=5 << 20, transcendentals=0
        ),
    )(columns, *weights, before)


def grad_kernel(columns_ref, upstream_ref, _, near_ref, far_ref):
    slots, tokens, width = columns_ref.shape
    half = width // 2
    upstream = upstream_ref[...]
    for index, out_ref in ((1, far_ref), (0, near_ref)):
        values = columns_ref[:, :, index * half:(index + 1) * half]
        out_ref[...] = lax.dot_general(
            values.reshape(slots * tokens, half),
            upstream,
            (((0,), (0,)), ((), ())),
            preferred_element_type=F32,
        )


def grad_products(columns, upstream, before):
    slots, tokens, width = columns.shape
    keys = upstream.shape[1]
    in_vmem = pl.BlockSpec(memory_space=pltpu.VMEM)
    return pl.pallas_call(
        grad_kernel,
        out_shape=[jax.ShapeDtypeStruct((width // 2, keys), F32)] * 2,
        in_specs=[in_vmem] * 2 + [pl.BlockSpec(memory_space=pl.ANY)],
        out_specs=[in_vmem] * 2,
        compiler_params=pltpu.CompilerParams(vmem_limit_bytes=VMEM_LIMIT),
        cost_estimate=pl.CostEstimate(
            flops=2 * slots * tokens * width * keys, bytes_accessed=6 << 20, transcendentals=0
        ),
    )(columns, upstream, before)


def term_kernel(near_ref, far_ref, near_weight_ref, far_weight_ref, out_ref):
    half = near_ref.shape[0]
    for index, (grad_ref, weight_ref) in enumerate(
        ((near_ref, near_weight_ref), (far_ref, far_weight_ref))
    ):
        products = grad_ref[...] * weight_ref[...].astype(F32)
        out_ref[:, index * half:(index + 1) * half] = lax.dot_general(
            jnp.ones((8, products.shape[1]), F32),
            products,
            (((1,), (1,)), ((), ())),
            precision=lax.Precision.HIGHEST,
            preferred_element_type=F32,
        )


def term_rows(near, far, weights):
    in_vmem = pl.BlockSpec(memory_space=pltpu.VMEM)
    return pl.pallas_call(
        term_kernel,
        out_shape=jax.ShapeDtypeStruct((8, 2 * near.shape[0]), F32),
        in_specs=[in_vmem] * 4,
        out_specs=in_vmem,
        compiler_params=pltpu.CompilerParams(vmem_limit_bytes=32 * 1024 * 1024),
        cost_estimate=pl.CostEstimate(
            flops=16 * near.size, bytes_accessed=4 << 20, transcendentals=0
        ),
    )(near, far, *weights)


def chip_kernel(near_ref, other_ref, terms_ref, own_ref, send_ref, terms_out):
    part = own_ref.shape[0]
    own_ref[...] = near_ref[:part] + other_ref[:part]
    send_ref[...] = (near_ref[part:] + other_ref[part:]).astype(BF16)
    terms_out[...] = terms_ref[...]


def chip_sums(near, other, terms):
    part, keys = near.shape[0] // 2, near.shape[1]
    return pl.pallas_call(
        chip_kernel,
        out_shape=(
            jax.ShapeDtypeStruct((part, keys), F32),
            jax.ShapeDtypeStruct((part, keys), BF16),
            jax.ShapeDtypeStruct(terms.shape, F32),
        ),
        compiler_params=pltpu.CompilerParams(vmem_limit_bytes=16 * 1024 * 1024),
        cost_estimate=pl.CostEstimate(
            flops=near.size, bytes_accessed=10 * near.size, transcendentals=0
        ),
    )(near, other, terms)


def swap(x, axis):
    return lax.ppermute(x, axis, [(0, 1), (1, 0)])


def halved(rows, axis, bit):
    half = rows.shape[0] // 2
    upper = (lax.axis_index(axis) & bit) != 0
    sent = jnp.where(upper, rows[:half], rows[half:])
    kept = jnp.where(upper, rows[half:], rows[:half])
    size = lax.axis_size(axis)
    received = lax.ppermute(sent, axis, [(i, i ^ bit) for i in range(size)])
    return kept.astype(F32) + received.astype(F32)


def body(
    activations, norm_gain, key_weight, key_cotangent, fragment_local, outer_params, outer_momentum
):
    slots = lax.axis_size("y")
    weight = key_weight[0]
    upstream = key_cotangent[0]
    part, keys = weight.shape
    tokens = upstream.shape[0]

    all_upstream = lax.all_gather(upstream, "y", axis=0, tiled=True)
    hidden = norm(activations[0], norm_gain, slots)
    columns = lax.all_to_all(hidden, "y", 0, 0, tiled=True)

    near_weight = jnp.concatenate([weight, swap(weight, "z")], axis=0)
    weights = [near_weight, swap(near_weight, "core")]

    own_share = fragment_local[0]
    for axis in REPLICA:
        for bit in (2, 1):
            own_share = halved(own_share, axis, bit)
    pseudo_grad = outer_params - own_share / (lax.axis_size("x") * lax.axis_size("depth"))
    new_momentum = 0.9 * outer_momentum + pseudo_grad
    new_params = outer_params - 0.7 * (pseudo_grad + 0.9 * new_momentum)

    key_terms = key_products(columns, weights, new_params)
    key_out = lax.psum_scatter(key_terms, "y", scatter_dimension=0, tiled=True).astype(BF16)

    near, far = grad_products(columns, all_upstream, key_terms)
    terms = term_rows(near, far, weights)
    own, send, terms = chip_sums(near, swap(far, "core"), terms)
    grad_rows = own + swap(send, "z").astype(F32)

    devices = 4 * slots
    spread = lax.all_to_all(
        jnp.broadcast_to(terms[:1], (devices, 4 * part)), FSDP, 0, 0, tiled=True
    ).reshape(2, slots, 2, 2, 2, part)
    total = [
        [
            sum(
                spread[a, :, b, core_to ^ b, z_to ^ a]
                for a in range(2)
                for b in range(2)
            )
            for core_to in range(2)
        ]
        for z_to in range(2)
    ]
    gain_total = jnp.stack([jnp.stack(t, axis=1) for t in total]).reshape(1, -1) / norm_gain
    return (key_out[None], grad_rows.astype(BF16)[None], gain_total, new_params, new_momentum)


def solution(mesh):
    replicas, devices = mesh.devices.shape
    split = Mesh(
        mesh.devices.reshape(replicas // 4, 4, 2, devices // 4, 2), REPLICA + FSDP
    )
    rows = P(REPLICA, FSDP, None)
    share = P(FSDP + REPLICA, None)
    return jax.shard_map(
        body,
        mesh=split,
        in_specs=(rows, P(REPLICA, None), rows, rows, rows, share, share),
        out_specs=(rows, rows, P(REPLICA, None), share, share),
        check_vma=False,
    )
```

```python
import jax
import jax.numpy as jnp
from jax import lax
from jax.experimental import pallas as pl
from jax.experimental.pallas import tpu as pltpu
from jax.sharding import Mesh, PartitionSpec as P

epsilon = 1e-05
F32 = jnp.float32
BF16 = jnp.bfloat16
REPLICA = ("x", "depth")
FSDP = ("z", "y", "core")
VMEM_LIMIT = 48 * 1024 * 1024
NORM_VMEM_LIMIT = 60 * 1024 * 1024


def norm_kernel(x_ref, gain_ref, out_ref):
    slots, _, width = out_ref.shape
    part = width // 4
    half = x_ref.shape[1] // 2
    values = x_ref[...].astype(F32)
    total = jnp.sum(values * values, axis=1, keepdims=True)
    inverse = lax.rsqrt(total / x_ref.shape[1] + epsilon)
    for slot in range(slots):
        for piece in range(4):
            z = lax.axis_index("z") ^ (piece & 1)
            core = lax.axis_index("core") ^ (piece >> 1)
            start = pl.multiple_of(z * half + slot * 2 * part + core * part, part)
            block = x_ref[:, pl.ds(start, part)].astype(F32)
            scale = gain_ref[:, pl.ds(start, part)]
            out_ref[slot, :, piece * part:(piece + 1) * part] = (
                (block * inverse) * scale
            ).astype(out_ref.dtype)


def norm(x, gain, slots):
    tokens, width = x.shape
    rows = 128
    return pl.pallas_call(
        norm_kernel,
        out_shape=jax.ShapeDtypeStruct((slots, tokens, width // slots), BF16),
        grid=(tokens // rows,),
        in_specs=[
            pl.BlockSpec((rows, width), lambda i: (i, 0)),
            pl.BlockSpec((1, width), lambda i: (0, 0)),
        ],
        out_specs=pl.BlockSpec((slots, rows, width // slots), lambda i: (0, i, 0)),
        compiler_params=pltpu.CompilerParams(vmem_limit_bytes=NORM_VMEM_LIMIT),
        cost_estimate=pl.CostEstimate(
            flops=6 * tokens * width, bytes_accessed=4 * tokens * width, transcendentals=tokens
        ),
    )(x, gain)


def key_kernel(columns_ref, near_ref, far_ref, _, out_ref):
    slots, tokens, width = columns_ref.shape
    weight = jnp.concatenate([near_ref[...], far_ref[...]], axis=0)
    terms = jnp.dot(
        columns_ref[...].reshape(slots * tokens, width), weight, preferred_element_type=F32
    )
    out_ref[...] = terms.astype(out_ref.dtype)


def key_products(columns, weights, before):
    slots, tokens, width = columns.shape
    keys = weights[0].shape[1]
    in_vmem = pl.BlockSpec(memory_space=pltpu.VMEM)
    return pl.pallas_call(
        key_kernel,
        out_shape=jax.ShapeDtypeStruct((slots * tokens, keys), BF16),
        in_specs=[in_vmem] * 3 + [pl.BlockSpec(memory_space=pl.ANY)],
        out_specs=in_vmem,
        compiler_params=pltpu.CompilerParams(vmem_limit_bytes=VMEM_LIMIT),
        cost_estimate=pl.CostEstimate(
            flops=2 * slots * tokens * width * keys, bytes_accessed=5 << 20, transcendentals=0
        ),
    )(columns, *weights, before)


def grad_kernel(columns_ref, upstream_ref, _, near_ref, far_ref):
    slots, tokens, width = columns_ref.shape
    half = width // 2
    upstream = upstream_ref[...]
    for index, out_ref in ((1, far_ref), (0, near_ref)):
        values = columns_ref[:, :, index * half:(index + 1) * half]
        out_ref[...] = lax.dot_general(
            values.reshape(slots * tokens, half),
            upstream,
            (((0,), (0,)), ((), ())),
            preferred_element_type=F32,
        )


def grad_products(columns, upstream, before):
    slots, tokens, width = columns.shape
    keys = upstream.shape[1]
    in_vmem = pl.BlockSpec(memory_space=pltpu.VMEM)
    return pl.pallas_call(
        grad_kernel,
        out_shape=[jax.ShapeDtypeStruct((width // 2, keys), F32)] * 2,
        in_specs=[in_vmem] * 2 + [pl.BlockSpec(memory_space=pl.ANY)],
        out_specs=[in_vmem] * 2,
        compiler_params=pltpu.CompilerParams(vmem_limit_bytes=VMEM_LIMIT),
        cost_estimate=pl.CostEstimate(
            flops=2 * slots * tokens * width * keys, bytes_accessed=6 << 20, transcendentals=0
        ),
    )(columns, upstream, before)


def term_kernel(near_ref, far_ref, near_weight_ref, far_weight_ref, out_ref):
    half = near_ref.shape[0]
    for index, (grad_ref, weight_ref) in enumerate(
        ((near_ref, near_weight_ref), (far_ref, far_weight_ref))
    ):
        products = grad_ref[...] * weight_ref[...].astype(F32)
        out_ref[:, index * half:(index + 1) * half] = lax.dot_general(
            jnp.ones((8, products.shape[1]), F32),
            products,
            (((1,), (1,)), ((), ())),
            precision=lax.Precision.HIGHEST,
            preferred_element_type=F32,
        )


def term_rows(near, far, weights):
    in_vmem = pl.BlockSpec(memory_space=pltpu.VMEM)
    return pl.pallas_call(
        term_kernel,
        out_shape=jax.ShapeDtypeStruct((8, 2 * near.shape[0]), F32),
        in_specs=[in_vmem] * 4,
        out_specs=in_vmem,
        compiler_params=pltpu.CompilerParams(vmem_limit_bytes=32 * 1024 * 1024),
        cost_estimate=pl.CostEstimate(
            flops=16 * near.size, bytes_accessed=4 << 20, transcendentals=0
        ),
    )(near, far, *weights)


def chip_kernel(near_ref, other_ref, terms_ref, own_ref, send_ref, terms_out):
    part = own_ref.shape[0]
    own_ref[...] = near_ref[:part] + other_ref[:part]
    send_ref[...] = (near_ref[part:] + other_ref[part:]).astype(BF16)
    terms_out[...] = terms_ref[...]


def chip_sums(near, other, terms):
    part, keys = near.shape[0] // 2, near.shape[1]
    return pl.pallas_call(
        chip_kernel,
        out_shape=(
            jax.ShapeDtypeStruct((part, keys), F32),
            jax.ShapeDtypeStruct((part, keys), BF16),
            jax.ShapeDtypeStruct(terms.shape, F32),
        ),
        compiler_params=pltpu.CompilerParams(vmem_limit_bytes=16 * 1024 * 1024),
        cost_estimate=pl.CostEstimate(
            flops=near.size, bytes_accessed=10 * near.size, transcendentals=0
        ),
    )(near, other, terms)


def swap(x, axis):
    return lax.ppermute(x, axis, [(0, 1), (1, 0)])


def halved(rows, axis, bit):
    half = rows.shape[0] // 2
    upper = (lax.axis_index(axis) & bit) != 0
    sent = jnp.where(upper, rows[:half], rows[half:])
    kept = jnp.where(upper, rows[half:], rows[:half])
    size = lax.axis_size(axis)
    received = lax.ppermute(sent, axis, [(i, i ^ bit) for i in range(size)])
    return kept.astype(F32) + received.astype(F32)


def body(
    activations, norm_gain, key_weight, key_cotangent, fragment_local, outer_params, outer_momentum
):
    slots = lax.axis_size("y")
    weight = key_weight[0]
    upstream = key_cotangent[0]
    part, keys = weight.shape
    tokens = upstream.shape[0]

    all_upstream = lax.all_gather(upstream, "y", axis=0, tiled=True)
    hidden = norm(activations[0], norm_gain, slots)
    columns = lax.all_to_all(hidden, "y", 0, 0, tiled=True)

    near_weight = jnp.concatenate([weight, swap(weight, "z")], axis=0)
    weights = [near_weight, swap(near_weight, "core")]

    own_share = fragment_local[0]
    for axis in REPLICA:
        for bit in (2, 1):
            own_share = halved(own_share, axis, bit)
    pseudo_grad = outer_params - own_share / (lax.axis_size("x") * lax.axis_size("depth"))
    new_momentum = 0.9 * outer_momentum + pseudo_grad
    new_params = outer_params - 0.7 * (pseudo_grad + 0.9 * new_momentum)

    key_terms = key_products(columns, weights, new_params)
    key_out = lax.psum_scatter(key_terms, "y", scatter_dimension=0, tiled=True).astype(BF16)

    near, far = grad_products(columns, all_upstream, key_terms)
    terms = term_rows(near, far, weights)
    own, send, terms = chip_sums(near, swap(far, "core"), terms)
    grad_rows = own + swap(send, "z").astype(F32)

    devices = 4 * slots
    spread = lax.all_to_all(
        jnp.broadcast_to(terms[:1], (devices, 4 * part)), FSDP, 0, 0, tiled=True
    ).reshape(2, slots, 2, 2, 2, part)
    total = [
        [
            sum(
                spread[a, :, b, core_to ^ b, z_to ^ a]
                for a in range(2)
                for b in range(2)
            )
            for core_to in range(2)
        ]
        for z_to in range(2)
    ]
    gain_total = jnp.stack([jnp.stack(t, axis=1) for t in total]).reshape(1, -1) / norm_gain
    return (key_out[None], grad_rows.astype(BF16)[None], gain_total, new_params, new_momentum)


def solution(mesh):
    replicas, devices = mesh.devices.shape
    split = Mesh(
        mesh.devices.reshape(replicas // 4, 4, 2, devices // 4, 2), REPLICA + FSDP
    )
    rows = P(REPLICA, FSDP, None)
    share = P(FSDP + REPLICA, None)
    return jax.shard_map(
        body,
        mesh=split,
        in_specs=(rows, P(REPLICA, None), rows, rows, rows, share, share),
        out_specs=(rows, rows, P(REPLICA, None), share, share),
        check_vma=False,
    )
```
